32 devices in a mesh: gz: 2 (over y), spec: 16 (over z, x, core).
Axes of the slice: x: 2, y: 2, z: 4, core: 2. Of those that a mesh axis runs over, the one named last changes fastest.
Arguments:
- flux: bfloat16 [4096, 7168], P('spec', 'gz'), may hold values from -6 to 6
- ivar: bfloat16 [4096, 7168], P('spec', 'gz'), may hold values from 0.25 to 4
- mask: int32 [4096, 7168], P('spec', 'gz'), may hold values 0 or 1
- table: bfloat16 [7168, 4, 256], P('spec', None, 'gz'), may hold values from -6 to 6
Outputs:
- decrease: float32 [4096, 256], P('spec', 'gz')
- best: float32 [4096], P('spec')
The draws below stay inside these ranges and needn't reach their ends.
Inputs may be any that keep to these rules, and one draw needn't show every extreme that they name: `mask`: 1 marks a good pixel, 0 a masked one.
All inputs are finite; a program needn't handle non-finite values. No bound on the sum of `mask` on one device may be relied on, other than what follows from the above.
Results may differ from the reference program's by a relative error of at most 0.0024.
Values may be sent and summed in bfloat16 or wider, within the bound.
A program may use at most 128 MiB of HBM per device.

```python
import math
import jax
import jax.numpy as jnp
from jax import lax

WAVE = 7168
COMP = 4
SDEV = 256
SPECTRA = 4096
ZGRID = 256


def with_ends(result, rng, low, high):
    longest = result.shape.index(max(result.shape))
    spots = []
    for shift in (0, 1):
        where = [jax.random.randint(jax.random.fold_in(rng, axis), (), 0, length) for axis, length in enumerate(result.shape)]
        where[longest] = (where[longest] + shift) % result.shape[longest]
        spots.append(tuple(where))
    return result.at[spots[0]].set(low).at[spots[1]].set(high)


def block_levels(key, dims, split, smallest, top_value):
    gain = 1.0
    for dim, shards_of in split:
        steps = jax.random.uniform(jax.random.fold_in(jax.random.fold_in(key, 6), dim), (shards_of,), jnp.float32, smallest / len(split), top_value / len(split))
        gain = gain * jnp.repeat(jnp.exp(steps), dims[dim] // shards_of).reshape((-1,) + (1,) * (len(dims) - 1 - dim))
    return gain


def noise(rng, dims, scale, bound, shards=(), kind=jnp.bfloat16):
    array = jax.random.normal(rng, dims, jnp.float32) * scale
    if len(shards) > 0:
        array = block_levels(rng, dims, shards, -0.22, 0.18) * array
    return jnp.clip(array, min=-bound, max=bound).astype(kind)


def setup_inputs(seed: int = 0) -> dict:
    keys = jax.random.split(jax.random.key(seed), 5)
    return {
        "flux": noise(keys[0], (SPECTRA, WAVE), 1.0, 6.0, ((0, 16), (1, 2))),
        "ivar": jnp.clip(jnp.exp(math.log(4.0) - 2.7725887 * jax.random.uniform(keys[1], (SPECTRA, WAVE), jnp.float32) ** block_levels(keys[1], (SPECTRA, WAVE), ((0, 16), (1, 2)), -0.2, 0.2)), 0.25, 4.0).astype(jnp.bfloat16),
        "mask": with_ends((jax.random.randint(keys[2], (SPECTRA, WAVE), 0, 8) < 7).astype(jnp.int32), jax.random.fold_in(keys[2], 1), 0, 1),
        "table": noise(keys[3], (WAVE, COMP, ZGRID), 1.0, 6.0, ((0, 16), (2, 2))),
    }


PAIR_LIST = ((0, 0), (0, 1), (0, 2), (0, 3), (1, 1), (1, 2), (1, 3), (2, 2), (2, 3), (3, 3))

def pair_table(templates):
    columns = [templates[:, i, :].astype(jnp.float32) * templates[:, j, :].astype(jnp.float32) for i, j in PAIR_LIST]
    return jnp.stack(columns, axis=1).astype(jnp.bfloat16)

def fit_gain(gram, proj):
    where = {}
    for number, pair in enumerate(PAIR_LIST):
        where[pair] = number
    lower = {}
    for j in range(4):
        diag = gram[:, where[j, j], :]
        for k in range(j):
            diag = diag - lower[j, k] * lower[j, k]
        lower[j, j] = jnp.sqrt(diag)
        for i in range(j + 1, 4):
            entry = gram[:, where[j, i], :]
            for k in range(j):
                entry = entry - lower[i, k] * lower[j, k]
            lower[i, j] = entry / lower[j, j]
    solved = []
    total = jnp.zeros(proj[:, 0, :].shape, jnp.float32)
    for i in range(4):
        value = proj[:, i, :]
        for k in range(i):
            value = value - lower[i, k] * solved[k]
        value = value / lower[i, i]
        solved.append(value)
        total = total + value * value
    return total

def reference(flux, ivar, mask, table):
    ivar_f = ivar.astype(jnp.float32)
    mask_f = mask.astype(jnp.float32)
    weight = (ivar_f * mask_f).astype(jnp.bfloat16)
    weighted = (flux.astype(jnp.float32) * ivar_f * mask_f).astype(jnp.bfloat16)
    wave_count = table.shape[0]
    grid = table.shape[2]
    flat_table = table.reshape(wave_count, 4 * grid)
    flat_pairs = pair_table(table).reshape(wave_count, 10 * grid)
    count = flux.shape[0]

    def one_block(block):
        part_weighted, part_weight = block
        proj = jnp.dot(part_weighted, flat_table, preferred_element_type=jnp.float32).reshape(-1, 4, grid)
        gram = jnp.dot(part_weight, flat_pairs, preferred_element_type=jnp.float32).reshape(-1, 10, grid)
        return fit_gain(gram, proj)
    blocks = (weighted.reshape(count // SDEV, SDEV, wave_count), weight.reshape(count // SDEV, SDEV, wave_count))
    decrease = lax.map(one_block, blocks).reshape(count, grid)
    best = lax.optimization_barrier(jnp.max(decrease, axis=1))
    return (decrease, best)
```

```python
import functools

import jax
import jax.numpy as jnp
from jax import lax
from jax.experimental import pallas as pl
from jax.experimental.pallas import tpu as pltpu
from jax.sharding import PartitionSpec as P

PAIR_LIST = ((0, 0), (0, 1), (0, 2), (0, 3), (1, 1), (1, 2), (1, 3), (2, 2), (2, 3), (3, 3))
MESH = pl.DeviceIdType.MESH
COMP = 4

STEPS = ((0, 0), (1, 0), (1, 1), (1, 2), (1, 3), (0, 1), (0, 2), (0, 3))


def pair_table(templates):
    columns = [
        templates[:, i, :].astype(jnp.float32) * templates[:, j, :].astype(jnp.float32)
        for i, j in PAIR_LIST
    ]
    return jnp.stack(columns, axis=1).astype(jnp.bfloat16)


def fit_gain(gram, proj):
    lower, inverse, solved, total = {}, [], [], None
    for j in range(COMP):
        diag = gram[j, j]
        for k in range(j):
            diag = diag - lower[j, k] * lower[j, k]
        inverse.append(lax.rsqrt(diag))
        for i in range(j + 1, COMP):
            entry = gram[j, i]
            for k in range(j):
                entry = entry - lower[i, k] * lower[j, k]
            lower[i, j] = entry * inverse[j]
        value = proj[j]
        for k in range(j):
            value = value - lower[j, k] * solved[k]
        value = value * inverse[j]
        solved.append(value)
        total = value * value if total is None else total + value * value
    return total


def gathered(flux, ivar, mask, table):
    ivar_f = ivar.astype(jnp.float32)
    mask_f = mask.astype(jnp.float32)
    weight = (ivar_f * mask_f).astype(jnp.bfloat16)
    weighted = (flux.astype(jnp.float32) * ivar_f * mask_f).astype(jnp.bfloat16)
    spectra_here = flux.shape[0]
    zlocal = table.shape[2]
    full_weighted = lax.all_gather(weighted, "gz", axis=1, tiled=True)
    full_weight = lax.all_gather(weight, "gz", axis=1, tiled=True)
    piece = lax.all_gather(table, "spec", axis=0, tiled=True)
    rows = piece.shape[0]
    flat_pairs = pair_table(piece).reshape(rows, 10 * zlocal)
    proj = jnp.dot(full_weighted, piece.reshape(rows, 4 * zlocal), preferred_element_type=jnp.float32)
    gram = jnp.dot(full_weight, flat_pairs, preferred_element_type=jnp.float32)
    proj = proj.reshape(spectra_here, 4, zlocal)
    gram = gram.reshape(spectra_here, 10, zlocal)
    decrease = fit_gain({p: gram[:, n] for n, p in enumerate(PAIR_LIST)}, [proj[:, k] for k in range(COMP)])
    return decrease, lax.pmax(jnp.max(decrease, axis=1), "gz")


def kernel(flux, ivar, mask, table, dec_ref, best_ref,
           flux_v, ivar_v, mask_v, weight, weighted, tbuf, pairs, gram_own, proj_own,
           gram_send, proj_send, gram_recv, proj_recv, top_send, top_recv,
           in_sem, recv_sem, up_sem, down_sem, x_sem, sib_sem, y_sem,
           part_send, part_recv, top_sems):
    y, s = lax.axis_index("gz"), lax.axis_index("spec")
    z, x, c = s // 4, lax.rem(s // 2, 2), lax.rem(s, 2)
    u = jnp.where(y == 0, z, 3 - z)
    dz = 1 - 2 * y
    spectra, waves = flux.shape
    blocks = tbuf.shape[2]

    def at(zz, xx, cc):
        return zz * 4 + xx * 2 + cc

    partner = (1 - y, s)
    sibling = (y, at(z, x, 1 - c))
    across = (y, at(z, 1 - x, c))
    up = (y, at(z + dz, x, c))
    down = (y, at(z - dz, x, c))

    loads = [
        pltpu.make_async_copy(ref, buf, in_sem.at[n])
        for n, (ref, buf) in enumerate(((flux, flux_v), (ivar, ivar_v), (mask, mask_v)))
    ]

    mine = at(z - 2 * y, x, c)
    theirs = at(z - 2 * (1 - y), x, c)

    def own_copy(k):
        return pltpu.make_async_copy(table.at[k], tbuf.at[0, k, mine], recv_sem.at[k, mine])

    def y_copy(k):
        return pltpu.make_async_remote_copy(
            src_ref=table.at[k], dst_ref=tbuf.at[1, k, theirs], send_sem=y_sem.at[k],
            recv_sem=recv_sem.at[COMP + k, theirs], device_id=partner, device_id_type=MESH)

    @pl.when(u <= 1)
    def _():
        for k in range(COMP):
            own_copy(k).start()

    barrier = pltpu.get_barrier_semaphore()
    for other in (partner, sibling, across):
        pl.semaphore_signal(barrier, inc=1, device_id=other, device_id_type=MESH)

    @pl.when(u <= 2)
    def _():
        pl.semaphore_signal(barrier, inc=1, device_id=up, device_id_type=MESH)

    @pl.when(u >= 1)
    def _():
        pl.semaphore_signal(barrier, inc=1, device_id=down, device_id_type=MESH)

    for load in loads:
        load.start()
    pl.semaphore_wait(barrier, jnp.where((u == 0) | (u == 3), 4, 5))

    @pl.when(u >= 2)
    def _():
        for k in range(COMP):
            y_copy(k).start()

    first = jnp.where(u >= 1, 1, 0)

    def block(j, xx, cc):
        v = first if j == 0 else 1 - first
        zrel = jnp.where(y == 0, v, 1 - v)
        return at(zrel, xx, cc)

    def arrived(t, b):
        w, k = STEPS[t]
        slot = tbuf.at[w, k, b]
        pltpu.make_async_copy(slot, slot, recv_sem.at[w * COMP + k, b]).wait()

    def forward(t, b, send_sem, to):
        w, k = STEPS[t]
        return pltpu.make_async_remote_copy(
            src_ref=tbuf.at[w, k, b], dst_ref=tbuf.at[w, k, b], send_sem=send_sem,
            recv_sem=recv_sem.at[w * COMP + k, b], device_id=to, device_id_type=MESH)

    def column_sends(t, j, do):
        b = block(j, x, c)

        @pl.when((u <= 2) if j == 0 else ((u == 1) | (u == 2)))
        def _():
            do(forward(t, b, up_sem.at[t, j], up))

        do(forward(t, b, x_sem.at[t, j], across))
        if j == 0:
            @pl.when(u == 1)
            def _():
                do(forward(t, b, down_sem.at[t], down))
        do(forward(t, b, sib_sem.at[t, j], sibling))

    def across_sends(t, j, do):
        do(forward(t, block(j, 1 - x, c), sib_sem.at[t, 2 + j], sibling))

    def column(t):
        for j in range(2):
            arrived(t, block(j, x, c))
            column_sends(t, j, lambda copy: copy.start())

    def neighbour(t):
        for j in range(2):
            arrived(t, block(j, 1 - x, c))
            across_sends(t, j, lambda copy: copy.start())

    def weights():
        for load in loads:
            load.wait()
        step = 32

        def body(n, carry):
            rows = pl.ds(pl.multiple_of(n * step, step), step)
            iv = ivar_v[rows, :].astype(jnp.float32)
            mk = mask_v[rows, :].astype(jnp.float32)
            weight[rows, :] = (iv * mk).astype(jnp.bfloat16)
            weighted[rows, :] = (flux_v[rows, :].astype(jnp.float32) * iv * mk).astype(jnp.bfloat16)
            return carry

        lax.fori_loop(0, spectra // step, body, 0)

    def part_copies(k):
        low = k * (k + 1) // 2
        refs = ((proj_send, proj_recv, pl.ds(k, 1)), (gram_send, gram_recv, pl.ds(low, k + 1)))
        return [
            pltpu.make_async_remote_copy(
                src_ref=src.at[rows], dst_ref=dst.at[rows], send_sem=part_send.at[k, n],
                recv_sem=part_recv.at[k, n], device_id=partner, device_id_type=MESH)
            for n, (src, dst, rows) in enumerate(refs)
        ]

    def compute(t):
        w, k = STEPS[t]
        for xx in range(2):
            for j in range(2):
                arrived(t, block(j, xx, 1 - c))
        for b in range(blocks):
            depth = tbuf.shape[3]
            rows = slice(b * depth, (b + 1) * depth)
            for i in range(k + 1):
                pairs[rows, i * 128:(i + 1) * 128] = tbuf[w, i, b] * tbuf[w, k, b]
        zlocal = tbuf.shape[4]
        proj = jnp.dot(weighted[...], tbuf[w, k].reshape(waves, zlocal), preferred_element_type=jnp.float32)
        gram = jnp.dot(weight[...], pairs[:, : (k + 1) * 128], preferred_element_type=jnp.float32)
        low = k * (k + 1) // 2
        if w == 0:
            proj_own[k] = proj
        else:
            proj_send[k] = proj
        for i in range(k + 1):
            part = gram[:, i * 128:(i + 1) * 128]
            if w == 0:
                gram_own[low + i] = part
            else:
                gram_send[low + i] = part.astype(jnp.bfloat16)
        if w == 1:
            for copy in part_copies(k):
                copy.start()

    count = len(STEPS)
    column(0)
    column(1)
    neighbour(0)
    weights()
    compute(0)
    for t in range(2, count):
        column(t)
        neighbour(t - 1)
        compute(t - 1)
    neighbour(count - 1)
    compute(count - 1)

    for k in range(COMP):
        for copy in part_copies(k):
            copy.wait_recv()
    step = 64

    def solve(n, carry):
        rows = pl.ds(pl.multiple_of(n * step, step), step)
        gram, proj = {}, []
        for k in range(COMP):
            proj.append(proj_own[k, rows, :] + proj_recv[k, rows, :])
            for i in range(k + 1):
                m = k * (k + 1) // 2 + i
                gram[i, k] = gram_own[m, rows, :] + gram_recv[m, rows, :].astype(jnp.float32)
        dec_ref[rows, :] = fit_gain(gram, proj)
        return carry

    lax.fori_loop(0, spectra // step, solve, 0)
    top = jnp.max(dec_ref[...].T, axis=0, keepdims=True)
    top_send[...] = jnp.broadcast_to(top, top_send.shape)
    top_copy = pltpu.make_async_remote_copy(
        src_ref=top_send, dst_ref=top_recv, send_sem=top_sems.at[0], recv_sem=top_sems.at[1],
        device_id=partner, device_id_type=MESH)
    top_copy.start()

    @pl.when(u >= 2)
    def _():
        for k in range(COMP):
            y_copy(k).wait_send()

    for t in range(count):
        for j in range(2):
            column_sends(t, j, lambda copy: copy.wait_send())
            across_sends(t, j, lambda copy: copy.wait_send())
    for k in range(COMP):
        for copy in part_copies(k):
            copy.wait_send()
    top_copy.wait()
    best_ref[...] = jnp.maximum(top_send[...], top_recv[...])


def fused(flux, ivar, mask, table):
    spectra, waves = flux.shape
    depth, comp, zlocal = table.shape
    pieces = comp * (comp + 1) // 2
    blocks = waves // depth
    by_component = table.transpose(1, 0, 2)
    bf16, f32 = jnp.bfloat16, jnp.float32
    dma = pltpu.SemaphoreType.DMA
    steps = len(STEPS)
    decrease, best = pl.pallas_call(
        kernel,
        out_shape=(
            jax.ShapeDtypeStruct((spectra, zlocal), f32),
            jax.ShapeDtypeStruct((8, spectra), f32),
        ),
        in_specs=[pl.BlockSpec(memory_space=pl.ANY)] * 4,
        out_specs=(pl.BlockSpec(memory_space=pltpu.VMEM), pl.BlockSpec(memory_space=pltpu.VMEM)),
        scratch_shapes=[
            pltpu.VMEM((spectra, waves), flux.dtype),
            pltpu.VMEM((spectra, waves), ivar.dtype),
            pltpu.VMEM((spectra, waves), mask.dtype),
            pltpu.VMEM((spectra, waves), bf16),
            pltpu.VMEM((spectra, waves), bf16),
            pltpu.VMEM((2, comp, blocks, depth, zlocal), bf16),
            pltpu.VMEM((waves, comp * zlocal), bf16),
            pltpu.VMEM((pieces, spectra, zlocal), f32),
            pltpu.VMEM((comp, spectra, zlocal), f32),
            pltpu.VMEM((pieces, spectra, zlocal), bf16),
            pltpu.VMEM((comp, spectra, zlocal), f32),
            pltpu.VMEM((pieces, spectra, zlocal), bf16),
            pltpu.VMEM((comp, spectra, zlocal), f32),
            pltpu.VMEM((8, spectra), f32),
            pltpu.VMEM((8, spectra), f32),
            dma((3,)),
            dma((steps, blocks)),
            dma((steps, 2)),
            dma((steps,)),
            dma((steps, 2)),
            dma((steps, 4)),
            dma((comp,)),
            dma((comp, 2)),
            dma((comp, 2)),
            dma((2,)),
        ],
        compiler_params=pltpu.CompilerParams(
            collective_id=0, has_side_effects=True, vmem_limit_bytes=48 * 1024 * 1024
        ),
        cost_estimate=pl.CostEstimate(
            flops=2 * spectra * waves * 2 * zlocal * (comp + pieces),
            bytes_accessed=8 * spectra * waves, transcendentals=0),
    )(flux, ivar, mask, by_component)
    return decrease, best[0]


def solution(mesh):
    placed = (P("spec", "gz"), P("spec", "gz"), P("spec", "gz"), P("spec", None, "gz"))
    local = fused if (mesh.shape["gz"], mesh.shape["spec"]) == (2, 16) else gathered
    return jax.shard_map(
        local, mesh=mesh, in_specs=placed, out_specs=(P("spec", "gz"), P("spec")), check_vma=False
    )
```

```python
import functools

import jax
import jax.numpy as jnp
from jax import lax
from jax.experimental import pallas as pl
from jax.experimental.pallas import tpu as pltpu
from jax.sharding import PartitionSpec as P

PAIR_LIST = ((0, 0), (0, 1), (0, 2), (0, 3), (1, 1), (1, 2), (1, 3), (2, 2), (2, 3), (3, 3))
MESH = pl.DeviceIdType.MESH
COMP = 4

STEPS = ((0, 0), (1, 0), (1, 1), (1, 2), (1, 3), (0, 1), (0, 2), (0, 3))


def pair_table(templates):
    columns = [
        templates[:, i, :].astype(jnp.float32) * templates[:, j, :].astype(jnp.float32)
        for i, j in PAIR_LIST
    ]
    return jnp.stack(columns, axis=1).astype(jnp.bfloat16)


def fit_gain(gram, proj):
    lower, inverse, solved, total = {}, [], [], None
    for j in range(COMP):
        diag = gram[j, j]
        for k in range(j):
            diag = diag - lower[j, k] * lower[j, k]
        inverse.append(lax.rsqrt(diag))
        for i in range(j + 1, COMP):
            entry = gram[j, i]
            for k in range(j):
                entry = entry - lower[i, k] * lower[j, k]
            lower[i, j] = entry * inverse[j]
        value = proj[j]
        for k in range(j):
            value = value - lower[j, k] * solved[k]
        value = value * inverse[j]
        solved.append(value)
        total = value * value if total is None else total + value * value
    return total


def gathered(flux, ivar, mask, table):
    ivar_f = ivar.astype(jnp.float32)
    mask_f = mask.astype(jnp.float32)
    weight = (ivar_f * mask_f).astype(jnp.bfloat16)
    weighted = (flux.astype(jnp.float32) * ivar_f * mask_f).astype(jnp.bfloat16)
    spectra_here = flux.shape[0]
    zlocal = table.shape[2]
    full_weighted = lax.all_gather(weighted, "gz", axis=1, tiled=True)
    full_weight = lax.all_gather(weight, "gz", axis=1, tiled=True)
    piece = lax.all_gather(table, "spec", axis=0, tiled=True)
    rows = piece.shape[0]
    flat_pairs = pair_table(piece).reshape(rows, 10 * zlocal)
    proj = jnp.dot(full_weighted, piece.reshape(rows, 4 * zlocal), preferred_element_type=jnp.float32)
    gram = jnp.dot(full_weight, flat_pairs, preferred_element_type=jnp.float32)
    proj = proj.reshape(spectra_here, 4, zlocal)
    gram = gram.reshape(spectra_here, 10, zlocal)
    decrease = fit_gain({p: gram[:, n] for n, p in enumerate(PAIR_LIST)}, [proj[:, k] for k in range(COMP)])
    return decrease, lax.pmax(jnp.max(decrease, axis=1), "gz")


def kernel(flux, ivar, mask, table, dec_ref, best_ref,
           flux_v, ivar_v, mask_v, weight, weighted, tbuf, pairs, gram_own, proj_own,
           gram_send, proj_send, gram_recv, proj_recv, top_send, top_recv,
           in_sem, recv_sem, up_sem, down_sem, x_sem, sib_sem, y_sem,
           part_send, part_recv, top_sems):
    y, s = lax.axis_index("gz"), lax.axis_index("spec")
    z, x, c = s // 4, lax.rem(s // 2, 2), lax.rem(s, 2)
    u = jnp.where(y == 0, z, 3 - z)
    dz = 1 - 2 * y
    spectra, waves = flux.shape
    blocks = tbuf.shape[2]

    def at(zz, xx, cc):
        return zz * 4 + xx * 2 + cc

    partner = (1 - y, s)
    sibling = (y, at(z, x, 1 - c))
    across = (y, at(z, 1 - x, c))
    up = (y, at(z + dz, x, c))
    down = (y, at(z - dz, x, c))

    loads = [
        pltpu.make_async_copy(ref, buf, in_sem.at[n])
        for n, (ref, buf) in enumerate(((flux, flux_v), (ivar, ivar_v), (mask, mask_v)))
    ]

    mine = at(z - 2 * y, x, c)
    theirs = at(z - 2 * (1 - y), x, c)

    def own_copy(k):
        return pltpu.make_async_copy(table.at[k], tbuf.at[0, k, mine], recv_sem.at[k, mine])

    def y_copy(k):
        return pltpu.make_async_remote_copy(
            src_ref=table.at[k], dst_ref=tbuf.at[1, k, theirs], send_sem=y_sem.at[k],
            recv_sem=recv_sem.at[COMP + k, theirs], device_id=partner, device_id_type=MESH)

    @pl.when(u <= 1)
    def _():
        for k in range(COMP):
            own_copy(k).start()

    barrier = pltpu.get_barrier_semaphore()
    for other in (partner, sibling, across):
        pl.semaphore_signal(barrier, inc=1, device_id=other, device_id_type=MESH)

    @pl.when(u <= 2)
    def _():
        pl.semaphore_signal(barrier, inc=1, device_id=up, device_id_type=MESH)

    @pl.when(u >= 1)
    def _():
        pl.semaphore_signal(barrier, inc=1, device_id=down, device_id_type=MESH)

    for load in loads:
        load.start()
    pl.semaphore_wait(barrier, jnp.where((u == 0) | (u == 3), 4, 5))

    def y_start(*which):
        @pl.when(u >= 2)
        def _():
            for k in which:
                y_copy(k).start()

    y_start(0, 1)

    first = jnp.where(u >= 1, 1, 0)
    count = len(STEPS)

    def block(j, xx, cc):
        v = first if j == 0 else 1 - first
        zrel = jnp.where(y == 0, v, 1 - v)
        return at(zrel, xx, cc)

    def arrived(t, b):
        w, k = STEPS[t]
        slot = tbuf.at[w, k, b]
        pltpu.make_async_copy(slot, slot, recv_sem.at[w * COMP + k, b]).wait()

    def forward(t, b, send_sem, to):
        w, k = STEPS[t]
        return pltpu.make_async_remote_copy(
            src_ref=tbuf.at[w, k, b], dst_ref=tbuf.at[w, k, b], send_sem=send_sem,
            recv_sem=recv_sem.at[w * COMP + k, b], device_id=to, device_id_type=MESH)

    def column_sends(t, j, do):
        b = block(j, x, c)

        @pl.when((u <= 2) if j == 0 else ((u == 1) | (u == 2)))
        def _():
            do(forward(t, b, up_sem.at[t, j], up))

        do(forward(t, b, x_sem.at[t, j], across))
        if j == 0:
            @pl.when(u == 1)
            def _():
                do(forward(t, b, down_sem.at[t], down))
        do(forward(t, b, sib_sem.at[t, j], sibling))

    def across_sends(t, j, do):
        do(forward(t, block(j, 1 - x, c), sib_sem.at[t, 2 + j], sibling))

    def column(t, j):
        if 0 <= t < count:
            arrived(t, block(j, x, c))
            column_sends(t, j, lambda copy: copy.start())

    def neighbour(t, j):
        if 0 <= t < count:
            arrived(t, block(j, 1 - x, c))
            across_sends(t, j, lambda copy: copy.start())

    def weights():
        for load in loads:
            load.wait()
        step = 32

        def body(n, carry):
            rows = pl.ds(pl.multiple_of(n * step, step), step)
            iv = ivar_v[rows, :].astype(jnp.float32)
            mk = mask_v[rows, :].astype(jnp.float32)
            weight[rows, :] = (iv * mk).astype(jnp.bfloat16)
            weighted[rows, :] = (flux_v[rows, :].astype(jnp.float32) * iv * mk).astype(jnp.bfloat16)
            return carry

        lax.fori_loop(0, spectra // step, body, 0)

    def part_copies(k):
        low = k * (k + 1) // 2
        refs = ((proj_send, proj_recv, pl.ds(k, 1)), (gram_send, gram_recv, pl.ds(low, k + 1)))
        return [
            pltpu.make_async_remote_copy(
                src_ref=src.at[rows], dst_ref=dst.at[rows], send_sem=part_send.at[k, n],
                recv_sem=part_recv.at[k, n], device_id=partner, device_id_type=MESH)
            for n, (src, dst, rows) in enumerate(refs)
        ]

    def compute(t, stage):
        if not 0 <= t < count:
            return
        w, k = STEPS[t]
        depth, zlocal = tbuf.shape[3:]
        low = k * (k + 1) // 2
        if stage == 0:
            for xx in range(2):
                for j in range(2):
                    arrived(t, block(j, xx, 1 - c))
        if stage < 2:
            for i in range(stage, k + 1, 2):
                for b in range(blocks):
                    pairs[b * depth:(b + 1) * depth, i * zlocal:(i + 1) * zlocal] = tbuf[w, i, b] * tbuf[w, k, b]
        if stage == 1:
            proj = jnp.dot(weighted[...], tbuf[w, k].reshape(waves, zlocal), preferred_element_type=jnp.float32)
            if w == 0:
                proj_own[k] = proj
            else:
                proj_send[k] = proj
        if stage >= 2:
            start = 2 * (stage - 2)
            stop = min(start + 2, k + 1)
            if start < stop:
                gram = jnp.dot(
                    weight[...], pairs[:, start * zlocal:stop * zlocal], preferred_element_type=jnp.float32)
                for i in range(start, stop):
                    part = gram[:, (i - start) * zlocal:(i - start + 1) * zlocal]
                    if w == 0:
                        gram_own[low + i] = part
                    else:
                        gram_send[low + i] = part.astype(jnp.bfloat16)
        if stage == 3 and w == 1:
            for copy in part_copies(k):
                copy.start()

    column(0, 0)
    y_start(2)
    for t in range(count + 2):
        column(t + 1, 0)
        if t == 0:
            y_start(3)
        compute(t - 2, 0)
        column(t, 1)
        compute(t - 2, 1)
        neighbour(t, 0)
        compute(t - 2, 2)
        neighbour(t - 1, 1)
        if t == 1:
            weights()
        compute(t - 2, 3)

    for k in range(COMP):
        for copy in part_copies(k):
            copy.wait_recv()
    step = 64

    def solve(n, carry):
        rows = pl.ds(pl.multiple_of(n * step, step), step)
        gram, proj = {}, []
        for k in range(COMP):
            proj.append(proj_own[k, rows, :] + proj_recv[k, rows, :])
            for i in range(k + 1):
                m = k * (k + 1) // 2 + i
                gram[i, k] = gram_own[m, rows, :] + gram_recv[m, rows, :].astype(jnp.float32)
        dec_ref[rows, :] = fit_gain(gram, proj)
        return carry

    lax.fori_loop(0, spectra // step, solve, 0)
    top = jnp.max(dec_ref[...].T, axis=0, keepdims=True)
    top_send[...] = jnp.broadcast_to(top, top_send.shape)
    top_copy = pltpu.make_async_remote_copy(
        src_ref=top_send, dst_ref=top_recv, send_sem=top_sems.at[0], recv_sem=top_sems.at[1],
        device_id=partner, device_id_type=MESH)
    top_copy.start()

    @pl.when(u >= 2)
    def _():
        for k in range(COMP):
            y_copy(k).wait_send()

    for t in range(count):
        for j in range(2):
            column_sends(t, j, lambda copy: copy.wait_send())
            across_sends(t, j, lambda copy: copy.wait_send())
    for k in range(COMP):
        for copy in part_copies(k):
            copy.wait_send()
    top_copy.wait()
    best_ref[...] = jnp.maximum(top_send[0:1, :], top_recv[0:1, :])


def fused(flux, ivar, mask, table):
    spectra, waves = flux.shape
    depth, comp, zlocal = table.shape
    pieces = comp * (comp + 1) // 2
    blocks = waves // depth
    by_component = table.transpose(1, 0, 2)
    bf16, f32 = jnp.bfloat16, jnp.float32
    dma = pltpu.SemaphoreType.DMA
    steps = len(STEPS)
    decrease, best = pl.pallas_call(
        kernel,
        out_shape=(
            jax.ShapeDtypeStruct((spectra, zlocal), f32),
            jax.ShapeDtypeStruct((1, spectra), f32),
        ),
        in_specs=[pl.BlockSpec(memory_space=pl.ANY)] * 4,
        out_specs=(pl.BlockSpec(memory_space=pltpu.VMEM), pl.BlockSpec(memory_space=pltpu.VMEM)),
        scratch_shapes=[
            pltpu.VMEM((spectra, waves), flux.dtype),
            pltpu.VMEM((spectra, waves), ivar.dtype),
            pltpu.VMEM((spectra, waves), mask.dtype),
            pltpu.VMEM((spectra, waves), bf16),
            pltpu.VMEM((spectra, waves), bf16),
            pltpu.VMEM((2, comp, blocks, depth, zlocal), bf16),
            pltpu.VMEM((waves, comp * zlocal), bf16),
            pltpu.VMEM((pieces, spectra, zlocal), f32),
            pltpu.VMEM((comp, spectra, zlocal), f32),
            pltpu.VMEM((pieces, spectra, zlocal), bf16),
            pltpu.VMEM((comp, spectra, zlocal), f32),
            pltpu.VMEM((pieces, spectra, zlocal), bf16),
            pltpu.VMEM((comp, spectra, zlocal), f32),
            pltpu.VMEM((8, spectra), f32),
            pltpu.VMEM((8, spectra), f32),
            dma((3,)),
            dma((steps, blocks)),
            dma((steps, 2)),
            dma((steps,)),
            dma((steps, 2)),
            dma((steps, 4)),
            dma((comp,)),
            dma((comp, 2)),
            dma((comp, 2)),
            dma((2,)),
        ],
        compiler_params=pltpu.CompilerParams(
            collective_id=0, has_side_effects=True, vmem_limit_bytes=63 * 1024 * 1024
        ),
        cost_estimate=pl.CostEstimate(
            flops=2 * spectra * waves * 2 * zlocal * (comp + pieces),
            bytes_accessed=8 * spectra * waves, transcendentals=0),
    )(flux, ivar, mask, by_component)
    return decrease, best.reshape(spectra)


def solution(mesh):
    placed = (P("spec", "gz"), P("spec", "gz"), P("spec", "gz"), P("spec", None, "gz"))
    local = fused if (mesh.shape["gz"], mesh.shape["spec"]) == (2, 16) else gathered
    return jax.shard_map(
        local, mesh=mesh, in_specs=placed, out_specs=(P("spec", "gz"), P("spec")), check_vma=False
    )
```

```python
import functools

import jax
import jax.numpy as jnp
from jax import lax
from jax.experimental import pallas as pl
from jax.experimental.pallas import tpu as pltpu
from jax.sharding import PartitionSpec as P

PAIR_LIST = ((0, 0), (0, 1), (0, 2), (0, 3), (1, 1), (1, 2), (1, 3), (2, 2), (2, 3), (3, 3))
MESH = pl.DeviceIdType.MESH
COMP = 4

STEPS = ((0, 0), (1, 0), (1, 1), (1, 2), (1, 3), (0, 1), (0, 2), (0, 3))
LAST_PARTS = 4


def pair_table(templates):
    columns = [
        templates[:, i, :].astype(jnp.float32) * templates[:, j, :].astype(jnp.float32)
        for i, j in PAIR_LIST
    ]
    return jnp.stack(columns, axis=1).astype(jnp.bfloat16)


def fit_gain(gram, proj):
    lower, inverse, solved, total = {}, [], [], None
    for j in range(COMP):
        diag = gram[j, j]
        for k in range(j):
            diag = diag - lower[j, k] * lower[j, k]
        inverse.append(lax.rsqrt(diag))
        for i in range(j + 1, COMP):
            entry = gram[j, i]
            for k in range(j):
                entry = entry - lower[i, k] * lower[j, k]
            lower[i, j] = entry * inverse[j]
        value = proj[j]
        for k in range(j):
            value = value - lower[j, k] * solved[k]
        value = value * inverse[j]
        solved.append(value)
        total = value * value if total is None else total + value * value
    return total


def gathered(flux, ivar, mask, table):
    ivar_f = ivar.astype(jnp.float32)
    mask_f = mask.astype(jnp.float32)
    weight = (ivar_f * mask_f).astype(jnp.bfloat16)
    weighted = (flux.astype(jnp.float32) * ivar_f * mask_f).astype(jnp.bfloat16)
    spectra_here = flux.shape[0]
    zlocal = table.shape[2]
    full_weighted = lax.all_gather(weighted, "gz", axis=1, tiled=True)
    full_weight = lax.all_gather(weight, "gz", axis=1, tiled=True)
    piece = lax.all_gather(table, "spec", axis=0, tiled=True)
    rows = piece.shape[0]
    flat_pairs = pair_table(piece).reshape(rows, 10 * zlocal)
    proj = jnp.dot(full_weighted, piece.reshape(rows, 4 * zlocal), preferred_element_type=jnp.float32)
    gram = jnp.dot(full_weight, flat_pairs, preferred_element_type=jnp.float32)
    proj = proj.reshape(spectra_here, 4, zlocal)
    gram = gram.reshape(spectra_here, 10, zlocal)
    decrease = fit_gain({p: gram[:, n] for n, p in enumerate(PAIR_LIST)}, [proj[:, k] for k in range(COMP)])
    return decrease, lax.pmax(jnp.max(decrease, axis=1), "gz")


def kernel(flux, ivar, mask, table, dec_ref, best_ref,
           flux_v, ivar_v, mask_v, weight, weighted, tbuf, pairs, gram_own, proj_own,
           gram_send, proj_send, gram_recv, proj_recv, top_send, top_recv,
           in_sem, recv_sem, up_sem, down_sem, x_sem, sib_sem, y_sem,
           part_send, part_recv, top_sems):
    y, s = lax.axis_index("gz"), lax.axis_index("spec")
    z, x, c = s // 4, lax.rem(s // 2, 2), lax.rem(s, 2)
    u = jnp.where(y == 0, z, 3 - z)
    dz = 1 - 2 * y
    spectra, waves = flux.shape
    blocks = tbuf.shape[2]

    def at(zz, xx, cc):
        return zz * 4 + xx * 2 + cc

    partner = (1 - y, s)
    sibling = (y, at(z, x, 1 - c))
    across = (y, at(z, 1 - x, c))
    up = (y, at(z + dz, x, c))
    down = (y, at(z - dz, x, c))

    loads = [
        pltpu.make_async_copy(ref, buf, in_sem.at[n])
        for n, (ref, buf) in enumerate(((flux, flux_v), (ivar, ivar_v), (mask, mask_v)))
    ]

    mine = at(z - 2 * y, x, c)
    theirs = at(z - 2 * (1 - y), x, c)

    count = len(STEPS)
    depth, zlocal = tbuf.shape[3:]

    def parts(w, k):
        return range(LAST_PARTS if (w, k) == STEPS[-1] else 1)

    def part_of(w, k, q):
        size = depth // len(parts(w, k))
        return pl.ds(q * size, size)

    def landed(w, k, b, q):
        return recv_sem.at[w * COMP + k if q == 0 else 2 * COMP + q - 1, b]

    def own_copy(k, q):
        rows = part_of(0, k, q)
        return pltpu.make_async_copy(table.at[k, rows], tbuf.at[0, k, mine, rows], landed(0, k, mine, q))

    def y_copy(k):
        return pltpu.make_async_remote_copy(
            src_ref=table.at[k], dst_ref=tbuf.at[1, k, theirs], send_sem=y_sem.at[k],
            recv_sem=recv_sem.at[COMP + k, theirs], device_id=partner, device_id_type=MESH)

    @pl.when(u <= 1)
    def _():
        for k in range(COMP):
            for q in parts(0, k):
                own_copy(k, q).start()

    barrier = pltpu.get_barrier_semaphore()
    for other in (partner, sibling, across):
        pl.semaphore_signal(barrier, inc=1, device_id=other, device_id_type=MESH)

    @pl.when(u <= 2)
    def _():
        pl.semaphore_signal(barrier, inc=1, device_id=up, device_id_type=MESH)

    @pl.when(u >= 1)
    def _():
        pl.semaphore_signal(barrier, inc=1, device_id=down, device_id_type=MESH)

    for load in loads:
        load.start()
    pl.semaphore_wait(barrier, jnp.where((u == 0) | (u == 3), 4, 5))

    def y_start(*which):
        @pl.when(u >= 2)
        def _():
            for k in which:
                y_copy(k).start()

    y_start(0, 1)

    first = jnp.where(u >= 1, 1, 0)

    def half(j):
        v = first if j == 0 else 1 - first
        return jnp.where(y == 0, v, 1 - v)

    def block(j, xx, cc):
        return at(half(j), xx, cc)

    def arrived(t, b, q):
        w, k = STEPS[t]
        slot = tbuf.at[w, k, b, part_of(w, k, q)]
        pltpu.make_async_copy(slot, slot, landed(w, k, b, q)).wait()

    def forward(t, b, q, send_sem, to):
        w, k = STEPS[t]
        slot = tbuf.at[w, k, b, part_of(w, k, q)]
        return pltpu.make_async_remote_copy(
            src_ref=slot, dst_ref=slot, send_sem=send_sem, recv_sem=landed(w, k, b, q),
            device_id=to, device_id_type=MESH)

    def column_sends(t, j, q, do):
        b, n = block(j, x, c), t + q

        @pl.when((u <= 2) if j == 0 else ((u == 1) | (u == 2)))
        def _():
            do(forward(t, b, q, up_sem.at[n, j], up))

        do(forward(t, b, q, x_sem.at[n, j], across))
        if j == 0:
            @pl.when(u == 1)
            def _():
                do(forward(t, b, q, down_sem.at[n], down))
        do(forward(t, b, q, sib_sem.at[n, j], sibling))

    def across_sends(t, j, q, do):
        do(forward(t, block(j, 1 - x, c), q, sib_sem.at[t + q, 2 + j], sibling))

    def column(t, j):
        if 0 <= t < count:
            for q in parts(*STEPS[t]):
                arrived(t, block(j, x, c), q)
                column_sends(t, j, q, lambda copy: copy.start())

    def neighbour(t, j):
        if 0 <= t < count:
            for q in parts(*STEPS[t]):
                arrived(t, block(j, 1 - x, c), q)
                across_sends(t, j, q, lambda copy: copy.start())

    def weights(stage):
        if stage == 0:
            for load in loads:
                load.wait()
        step = 32
        some = spectra // step // 4

        def body(n, carry):
            rows = pl.ds(pl.multiple_of(n * step, step), step)
            iv = ivar_v[rows, :].astype(jnp.float32)
            mk = mask_v[rows, :].astype(jnp.float32)
            weight[rows, :] = (iv * mk).astype(jnp.bfloat16)
            weighted[rows, :] = (flux_v[rows, :].astype(jnp.float32) * iv * mk).astype(jnp.bfloat16)
            return carry

        lax.fori_loop(stage * some, (stage + 1) * some, body, 0)

    def part_copies(k):
        low = k * (k + 1) // 2
        refs = ((proj_send, proj_recv, pl.ds(k, 1)), (gram_send, gram_recv, pl.ds(low, k + 1)))
        return [
            pltpu.make_async_remote_copy(
                src_ref=src.at[rows], dst_ref=dst.at[rows], send_sem=part_send.at[k, n],
                recv_sem=part_recv.at[k, n], device_id=partner, device_id_type=MESH)
            for n, (src, dst, rows) in enumerate(refs)
        ]

    def compute(t, stage):
        if t == -1:
            weights(stage)
        if not 0 <= t < count - 1:
            return
        w, k = STEPS[t]
        low = k * (k + 1) // 2
        if stage == 0:
            for xx in range(2):
                for j in range(2):
                    arrived(t, block(j, xx, 1 - c), 0)
        if stage < 2:
            for i in range(stage, k + 1, 2):
                for b in range(blocks):
                    pairs[b * depth:(b + 1) * depth, i * zlocal:(i + 1) * zlocal] = tbuf[w, i, b] * tbuf[w, k, b]
        if stage == 1:
            proj = jnp.dot(weighted[...], tbuf[w, k].reshape(waves, zlocal), preferred_element_type=jnp.float32)
            if w == 0:
                proj_own[k] = proj
            else:
                proj_send[k] = proj
        if stage >= 2:
            start = 2 * (stage - 2)
            stop = min(start + 2, k + 1)
            if start < stop:
                gram = jnp.dot(
                    weight[...], pairs[:, start * zlocal:stop * zlocal], preferred_element_type=jnp.float32)
                for i in range(start, stop):
                    part = gram[:, (i - start) * zlocal:(i - start + 1) * zlocal]
                    if w == 0:
                        gram_own[low + i] = part
                    else:
                        gram_send[low + i] = part.astype(jnp.bfloat16)
        if stage == 3 and w == 1:
            for copy in part_copies(k):
                copy.start()

    def compute_last(j):
        w, k = STEPS[-1]
        low = k * (k + 1) // 2
        for xx in range(2):
            for q in parts(w, k):
                arrived(count - 1, block(j, xx, 1 - c), q)
        some, size = blocks // 2, waves // 2
        base = half(j) * some
        columns = pl.ds(pl.multiple_of(half(j) * size, 128), size)
        for i in range(k + 1):
            for n in range(some):
                pairs[n * depth:(n + 1) * depth, i * zlocal:(i + 1) * zlocal] = (
                    tbuf[w, i, base + n] * tbuf[w, k, base + n])
        new = tbuf[w, k, pl.ds(base, some)].reshape(size, zlocal)
        proj = jnp.dot(weighted[:, columns], new, preferred_element_type=jnp.float32)
        proj_own[k] = proj if j == 0 else proj_own[k] + proj
        gram = jnp.dot(weight[:, columns], pairs[:size, :(k + 1) * zlocal], preferred_element_type=jnp.float32)
        for i in range(k + 1):
            part = gram[:, i * zlocal:(i + 1) * zlocal]
            gram_own[low + i] = part if j == 0 else gram_own[low + i] + part

    column(0, 0)
    y_start(2)
    for t in range(count):
        column(t + 1, 0)
        if t == 0:
            y_start(3)
        compute(t - 2, 0)
        column(t, 1)
        compute(t - 2, 1)
        neighbour(t, 0)
        compute(t - 2, 2)
        neighbour(t - 1, 1)
        compute(t - 2, 3)
    compute(count - 2, 0)
    compute(count - 2, 1)
    neighbour(count - 1, 1)
    compute(count - 2, 2)
    compute(count - 2, 3)
    compute_last(0)
    compute_last(1)

    for k in range(COMP):
        for copy in part_copies(k):
            copy.wait_recv()
    step = 64

    def solve(n, carry):
        rows = pl.ds(pl.multiple_of(n * step, step), step)
        gram, proj = {}, []
        for k in range(COMP):
            proj.append(proj_own[k, rows, :] + proj_recv[k, rows, :])
            for i in range(k + 1):
                m = k * (k + 1) // 2 + i
                gram[i, k] = gram_own[m, rows, :] + gram_recv[m, rows, :].astype(jnp.float32)
        dec_ref[rows, :] = fit_gain(gram, proj)
        return carry

    lax.fori_loop(0, spectra // step, solve, 0)
    top = jnp.max(dec_ref[...].T, axis=0, keepdims=True)
    top_send[...] = jnp.broadcast_to(top, top_send.shape)
    top_copy = pltpu.make_async_remote_copy(
        src_ref=top_send, dst_ref=top_recv, send_sem=top_sems.at[0], recv_sem=top_sems.at[1],
        device_id=partner, device_id_type=MESH)
    top_copy.start()

    @pl.when(u >= 2)
    def _():
        for k in range(COMP):
            y_copy(k).wait_send()

    for t in range(count):
        for j in range(2):
            for q in parts(*STEPS[t]):
                column_sends(t, j, q, lambda copy: copy.wait_send())
                across_sends(t, j, q, lambda copy: copy.wait_send())
    for k in range(COMP):
        for copy in part_copies(k):
            copy.wait_send()
    top_copy.wait()
    best_ref[...] = jnp.maximum(top_send[0:1, :], top_recv[0:1, :])


def fused(flux, ivar, mask, table):
    spectra, waves = flux.shape
    depth, comp, zlocal = table.shape
    pieces = comp * (comp + 1) // 2
    blocks = waves // depth
    by_component = table.transpose(1, 0, 2)
    bf16, f32 = jnp.bfloat16, jnp.float32
    dma = pltpu.SemaphoreType.DMA
    steps = len(STEPS)
    decrease, best = pl.pallas_call(
        kernel,
        out_shape=(
            jax.ShapeDtypeStruct((spectra, zlocal), f32),
            jax.ShapeDtypeStruct((1, spectra), f32),
        ),
        in_specs=[pl.BlockSpec(memory_space=pl.ANY)] * 4,
        out_specs=(pl.BlockSpec(memory_space=pltpu.VMEM), pl.BlockSpec(memory_space=pltpu.VMEM)),
        scratch_shapes=[
            pltpu.VMEM((spectra, waves), flux.dtype),
            pltpu.VMEM((spectra, waves), ivar.dtype),
            pltpu.VMEM((spectra, waves), mask.dtype),
            pltpu.VMEM((spectra, waves), bf16),
            pltpu.VMEM((spectra, waves), bf16),
            pltpu.VMEM((2, comp, blocks, depth, zlocal), bf16),
            pltpu.VMEM((waves, comp * zlocal), bf16),
            pltpu.VMEM((pieces, spectra, zlocal), f32),
            pltpu.VMEM((comp, spectra, zlocal), f32),
            pltpu.VMEM((pieces, spectra, zlocal), bf16),
            pltpu.VMEM((comp, spectra, zlocal), f32),
            pltpu.VMEM((pieces, spectra, zlocal), bf16),
            pltpu.VMEM((comp, spectra, zlocal), f32),
            pltpu.VMEM((8, spectra), f32),
            pltpu.VMEM((8, spectra), f32),
            dma((3,)),
            dma((2 * comp + LAST_PARTS - 1, blocks)),
            dma((steps + LAST_PARTS - 1, 2)),
            dma((steps + LAST_PARTS - 1,)),
            dma((steps + LAST_PARTS - 1, 2)),
            dma((steps + LAST_PARTS - 1, 4)),
            dma((comp,)),
            dma((comp, 2)),
            dma((comp, 2)),
            dma((2,)),
        ],
        compiler_params=pltpu.CompilerParams(
            collective_id=0, has_side_effects=True, vmem_limit_bytes=123 * 512 * 1024
        ),
        cost_estimate=pl.CostEstimate(
            flops=2 * spectra * waves * 2 * zlocal * (comp + pieces),
            bytes_accessed=8 * spectra * waves, transcendentals=0),
    )(flux, ivar, mask, by_component)
    return decrease, best.reshape(spectra)


def solution(mesh):
    placed = (P("spec", "gz"), P("spec", "gz"), P("spec", "gz"), P("spec", None, "gz"))
    local = fused if (mesh.shape["gz"], mesh.shape["spec"]) == (2, 16) else gathered
    return jax.shard_map(
        local, mesh=mesh, in_specs=placed, out_specs=(P("spec", "gz"), P("spec")), check_vma=False
    )
```

```python
import functools

import jax
import jax.numpy as jnp
from jax import lax
from jax.experimental import pallas as pl
from jax.experimental.pallas import tpu as pltpu
from jax.sharding import PartitionSpec as P

PAIR_LIST = ((0, 0), (0, 1), (0, 2), (0, 3), (1, 1), (1, 2), (1, 3), (2, 2), (2, 3), (3, 3))
MESH = pl.DeviceIdType.MESH
COMP = 4

STEPS = ((1, 0), (1, 1), (1, 2), (1, 3), (0, 0), (0, 1), (0, 2), (0, 3))
LAST_PARTS = 4


def pair_table(templates):
    columns = [
        templates[:, i, :].astype(jnp.float32) * templates[:, j, :].astype(jnp.float32)
        for i, j in PAIR_LIST
    ]
    return jnp.stack(columns, axis=1).astype(jnp.bfloat16)


def fit_gain(gram, proj):
    lower, inverse, solved, total = {}, [], [], None
    for j in range(COMP):
        diag = gram[j, j]
        for k in range(j):
            diag = diag - lower[j, k] * lower[j, k]
        inverse.append(lax.rsqrt(diag))
        for i in range(j + 1, COMP):
            entry = gram[j, i]
            for k in range(j):
                entry = entry - lower[i, k] * lower[j, k]
            lower[i, j] = entry * inverse[j]
        value = proj[j]
        for k in range(j):
            value = value - lower[j, k] * solved[k]
        value = value * inverse[j]
        solved.append(value)
        total = value * value if total is None else total + value * value
    return total


def gathered(flux, ivar, mask, table):
    ivar_f = ivar.astype(jnp.float32)
    mask_f = mask.astype(jnp.float32)
    weight = (ivar_f * mask_f).astype(jnp.bfloat16)
    weighted = (flux.astype(jnp.float32) * ivar_f * mask_f).astype(jnp.bfloat16)
    spectra_here = flux.shape[0]
    zlocal = table.shape[2]
    full_weighted = lax.all_gather(weighted, "gz", axis=1, tiled=True)
    full_weight = lax.all_gather(weight, "gz", axis=1, tiled=True)
    piece = lax.all_gather(table, "spec", axis=0, tiled=True)
    rows = piece.shape[0]
    flat_pairs = pair_table(piece).reshape(rows, 10 * zlocal)
    proj = jnp.dot(full_weighted, piece.reshape(rows, 4 * zlocal), preferred_element_type=jnp.float32)
    gram = jnp.dot(full_weight, flat_pairs, preferred_element_type=jnp.float32)
    proj = proj.reshape(spectra_here, 4, zlocal)
    gram = gram.reshape(spectra_here, 10, zlocal)
    decrease = fit_gain({p: gram[:, n] for n, p in enumerate(PAIR_LIST)}, [proj[:, k] for k in range(COMP)])
    return decrease, lax.pmax(jnp.max(decrease, axis=1), "gz")


def kernel(flux, ivar, mask, table, dec_ref, best_ref,
           flux_v, ivar_v, mask_v, weight, weighted, tbuf, pairs, gram_own, proj_own,
           gram_send, proj_send, gram_recv, proj_recv, top_send, top_recv,
           in_sem, recv_sem, up_sem, down_sem, x_sem, sib_sem, y_sem,
           part_send, part_recv, top_sems):
    y, s = lax.axis_index("gz"), lax.axis_index("spec")
    z, x, c = s // 4, lax.rem(s // 2, 2), lax.rem(s, 2)
    u = jnp.where(y == 0, z, 3 - z)
    dz = 1 - 2 * y
    spectra, waves = flux.shape
    blocks = tbuf.shape[2]

    def at(zz, xx, cc):
        return zz * 4 + xx * 2 + cc

    partner = (1 - y, s)
    sibling = (y, at(z, x, 1 - c))
    across = (y, at(z, 1 - x, c))
    up = (y, at(z + dz, x, c))
    down = (y, at(z - dz, x, c))

    loads = [
        pltpu.make_async_copy(ref, buf, in_sem.at[n])
        for n, (ref, buf) in enumerate(((flux, flux_v), (ivar, ivar_v), (mask, mask_v)))
    ]

    mine = at(z - 2 * y, x, c)
    theirs = at(z - 2 * (1 - y), x, c)

    count = len(STEPS)
    depth, zlocal = tbuf.shape[3:]

    def parts(w, k):
        return range(LAST_PARTS if (w, k) == STEPS[-1] else 1)

    def part_of(w, k, q):
        size = depth // len(parts(w, k))
        return pl.ds(q * size, size)

    def landed(w, k, b, q):
        return recv_sem.at[w * COMP + k if q == 0 else 2 * COMP + q - 1, b]

    def own_copy(k, q):
        rows = part_of(0, k, q)
        return pltpu.make_async_copy(table.at[k, rows], tbuf.at[0, k, mine, rows], landed(0, k, mine, q))

    def y_copy(k):
        return pltpu.make_async_remote_copy(
            src_ref=table.at[k], dst_ref=tbuf.at[1, k, theirs], send_sem=y_sem.at[k],
            recv_sem=recv_sem.at[COMP + k, theirs], device_id=partner, device_id_type=MESH)

    @pl.when(u <= 1)
    def _():
        for k in range(COMP):
            for q in parts(0, k):
                own_copy(k, q).start()

    barrier = pltpu.get_barrier_semaphore()
    for other in (partner, sibling, across):
        pl.semaphore_signal(barrier, inc=1, device_id=other, device_id_type=MESH)

    @pl.when(u <= 2)
    def _():
        pl.semaphore_signal(barrier, inc=1, device_id=up, device_id_type=MESH)

    @pl.when(u >= 1)
    def _():
        pl.semaphore_signal(barrier, inc=1, device_id=down, device_id_type=MESH)

    for load in loads:
        load.start()
    pl.semaphore_wait(barrier, jnp.where((u == 0) | (u == 3), 4, 5))

    def y_start(*which):
        @pl.when(u >= 2)
        def _():
            for k in which:
                y_copy(k).start()

    y_start(0, 1, 2)

    first = jnp.where(u >= 1, 1, 0)

    def half(j):
        v = first if j == 0 else 1 - first
        return jnp.where(y == 0, v, 1 - v)

    def block(j, xx, cc):
        return at(half(j), xx, cc)

    def arrived(t, b, q):
        w, k = STEPS[t]
        slot = tbuf.at[w, k, b, part_of(w, k, q)]
        pltpu.make_async_copy(slot, slot, landed(w, k, b, q)).wait()

    def forward(t, b, q, send_sem, to):
        w, k = STEPS[t]
        slot = tbuf.at[w, k, b, part_of(w, k, q)]
        return pltpu.make_async_remote_copy(
            src_ref=slot, dst_ref=slot, send_sem=send_sem, recv_sem=landed(w, k, b, q),
            device_id=to, device_id_type=MESH)

    def column_sends(t, j, q, do):
        b, n = block(j, x, c), t + q

        @pl.when((u <= 2) if j == 0 else ((u == 1) | (u == 2)))
        def _():
            do(forward(t, b, q, up_sem.at[n, j], up))

        do(forward(t, b, q, x_sem.at[n, j], across))
        if j == 0:
            @pl.when(u == 1)
            def _():
                do(forward(t, b, q, down_sem.at[n], down))
        do(forward(t, b, q, sib_sem.at[n, j], sibling))

    def across_sends(t, j, q, do):
        do(forward(t, block(j, 1 - x, c), q, sib_sem.at[t + q, 2 + j], sibling))

    def column(t, j):
        if 0 <= t < count:
            for q in parts(*STEPS[t]):
                arrived(t, block(j, x, c), q)
                column_sends(t, j, q, lambda copy: copy.start())

    def neighbour(t, j):
        if 0 <= t < count:
            for q in parts(*STEPS[t]):
                arrived(t, block(j, 1 - x, c), q)
                across_sends(t, j, q, lambda copy: copy.start())

    def weights(stage):
        if stage == 0:
            for load in loads:
                load.wait()
        step = 32
        some = spectra // step // 4

        def body(n, carry):
            rows = pl.ds(pl.multiple_of(n * step, step), step)
            iv = ivar_v[rows, :].astype(jnp.float32)
            mk = mask_v[rows, :].astype(jnp.float32)
            weight[rows, :] = (iv * mk).astype(jnp.bfloat16)
            weighted[rows, :] = (flux_v[rows, :].astype(jnp.float32) * iv * mk).astype(jnp.bfloat16)
            return carry

        lax.fori_loop(stage * some, (stage + 1) * some, body, 0)

    def part_copies(k):
        low = k * (k + 1) // 2
        refs = ((proj_send, proj_recv, pl.ds(k, 1)), (gram_send, gram_recv, pl.ds(low, k + 1)))
        return [
            pltpu.make_async_remote_copy(
                src_ref=src.at[rows], dst_ref=dst.at[rows], send_sem=part_send.at[k, n],
                recv_sem=part_recv.at[k, n], device_id=partner, device_id_type=MESH)
            for n, (src, dst, rows) in enumerate(refs)
        ]

    def compute(t, stage):
        if t == -1:
            weights(stage)
        if not 0 <= t < count - 1:
            return
        w, k = STEPS[t]
        low = k * (k + 1) // 2
        if stage == 0:
            for xx in range(2):
                for j in range(2):
                    arrived(t, block(j, xx, 1 - c), 0)
        if stage < 2:
            for i in range(stage, k + 1, 2):
                for b in range(blocks):
                    pairs[b * depth:(b + 1) * depth, i * zlocal:(i + 1) * zlocal] = tbuf[w, i, b] * tbuf[w, k, b]
        if stage == 1:
            proj = jnp.dot(weighted[...], tbuf[w, k].reshape(waves, zlocal), preferred_element_type=jnp.float32)
            if w == 0:
                proj_own[k] = proj
            else:
                proj_send[k] = proj
        if stage >= 2:
            start = 2 * (stage - 2)
            stop = min(start + 2, k + 1)
            if start < stop:
                gram = jnp.dot(
                    weight[...], pairs[:, start * zlocal:stop * zlocal], preferred_element_type=jnp.float32)
                for i in range(start, stop):
                    part = gram[:, (i - start) * zlocal:(i - start + 1) * zlocal]
                    if w == 0:
                        gram_own[low + i] = part
                    else:
                        gram_send[low + i] = part.astype(jnp.bfloat16)
        if stage == 3 and w == 1:
            for copy in part_copies(k):
                copy.start()

    def compute_last(j):
        w, k = STEPS[-1]
        low = k * (k + 1) // 2
        for xx in range(2):
            for q in parts(w, k):
                arrived(count - 1, block(j, xx, 1 - c), q)
        some, size = blocks // 2, waves // 2
        base = half(j) * some
        columns = pl.ds(pl.multiple_of(half(j) * size, 128), size)
        for i in range(k + 1):
            for n in range(some):
                pairs[n * depth:(n + 1) * depth, i * zlocal:(i + 1) * zlocal] = (
                    tbuf[w, i, base + n] * tbuf[w, k, base + n])
        new = tbuf[w, k, pl.ds(base, some)].reshape(size, zlocal)
        proj = jnp.dot(weighted[:, columns], new, preferred_element_type=jnp.float32)
        proj_own[k] = proj if j == 0 else proj_own[k] + proj
        gram = jnp.dot(weight[:, columns], pairs[:size, :(k + 1) * zlocal], preferred_element_type=jnp.float32)
        for i in range(k + 1):
            part = gram[:, i * zlocal:(i + 1) * zlocal]
            gram_own[low + i] = part if j == 0 else gram_own[low + i] + part

    column(0, 0)
    y_start(3)
    for t in range(count):
        column(t + 1, 0)
        compute(t - 2, 0)
        column(t, 1)
        compute(t - 2, 1)
        neighbour(t, 0)
        compute(t - 2, 2)
        neighbour(t - 1, 1)
        compute(t - 2, 3)
    compute(count - 2, 0)
    compute(count - 2, 1)
    neighbour(count - 1, 1)
    compute(count - 2, 2)
    compute(count - 2, 3)
    compute_last(0)
    compute_last(1)

    for k in range(COMP):
        for copy in part_copies(k):
            copy.wait_recv()
    step = 64

    def solve(n, carry):
        rows = pl.ds(pl.multiple_of(n * step, step), step)
        gram, proj = {}, []
        for k in range(COMP):
            proj.append(proj_own[k, rows, :] + proj_recv[k, rows, :])
            for i in range(k + 1):
                m = k * (k + 1) // 2 + i
                gram[i, k] = gram_own[m, rows, :] + gram_recv[m, rows, :].astype(jnp.float32)
        dec_ref[rows, :] = fit_gain(gram, proj)
        return carry

    lax.fori_loop(0, spectra // step, solve, 0)
    top = jnp.max(dec_ref[...].T, axis=0, keepdims=True)
    top_send[...] = jnp.broadcast_to(top, top_send.shape)
    top_copy = pltpu.make_async_remote_copy(
        src_ref=top_send, dst_ref=top_recv, send_sem=top_sems.at[0], recv_sem=top_sems.at[1],
        device_id=partner, device_id_type=MESH)
    top_copy.start()

    @pl.when(u >= 2)
    def _():
        for k in range(COMP):
            y_copy(k).wait_send()

    for t in range(count):
        for j in range(2):
            for q in parts(*STEPS[t]):
                column_sends(t, j, q, lambda copy: copy.wait_send())
                across_sends(t, j, q, lambda copy: copy.wait_send())
    for k in range(COMP):
        for copy in part_copies(k):
            copy.wait_send()
    top_copy.wait()
    best_ref[...] = jnp.maximum(top_send[0:1, :], top_recv[0:1, :])


def fused(flux, ivar, mask, table):
    spectra, waves = flux.shape
    depth, comp, zlocal = table.shape
    pieces = comp * (comp + 1) // 2
    blocks = waves // depth
    by_component = table.transpose(1, 0, 2)
    bf16, f32 = jnp.bfloat16, jnp.float32
    dma = pltpu.SemaphoreType.DMA
    steps = len(STEPS)
    decrease, best = pl.pallas_call(
        kernel,
        out_shape=(
            jax.ShapeDtypeStruct((spectra, zlocal), f32),
            jax.ShapeDtypeStruct((1, spectra), f32),
        ),
        in_specs=[pl.BlockSpec(memory_space=pl.ANY)] * 4,
        out_specs=(pl.BlockSpec(memory_space=pltpu.VMEM), pl.BlockSpec(memory_space=pltpu.VMEM)),
        scratch_shapes=[
            pltpu.VMEM((spectra, waves), flux.dtype),
            pltpu.VMEM((spectra, waves), ivar.dtype),
            pltpu.VMEM((spectra, waves), mask.dtype),
            pltpu.VMEM((spectra, waves), bf16),
            pltpu.VMEM((spectra, waves), bf16),
            pltpu.VMEM((2, comp, blocks, depth, zlocal), bf16),
            pltpu.VMEM((waves, comp * zlocal), bf16),
            pltpu.VMEM((pieces, spectra, zlocal), f32),
            pltpu.VMEM((comp, spectra, zlocal), f32),
            pltpu.VMEM((pieces, spectra, zlocal), bf16),
            pltpu.VMEM((comp, spectra, zlocal), f32),
            pltpu.VMEM((pieces, spectra, zlocal), bf16),
            pltpu.VMEM((comp, spectra, zlocal), f32),
            pltpu.VMEM((8, spectra), f32),
            pltpu.VMEM((8, spectra), f32),
            dma((3,)),
            dma((2 * comp + LAST_PARTS - 1, blocks)),
            dma((steps + LAST_PARTS - 1, 2)),
            dma((steps + LAST_PARTS - 1,)),
            dma((steps + LAST_PARTS - 1, 2)),
            dma((steps + LAST_PARTS - 1, 4)),
            dma((comp,)),
            dma((comp, 2)),
            dma((comp, 2)),
            dma((2,)),
        ],
        compiler_params=pltpu.CompilerParams(
            collective_id=0, has_side_effects=True, vmem_limit_bytes=123 * 512 * 1024
        ),
        cost_estimate=pl.CostEstimate(
            flops=2 * spectra * waves * 2 * zlocal * (comp + pieces),
            bytes_accessed=8 * spectra * waves, transcendentals=0),
    )(flux, ivar, mask, by_component)
    return decrease, best.reshape(spectra)


def solution(mesh):
    placed = (P("spec", "gz"), P("spec", "gz"), P("spec", "gz"), P("spec", None, "gz"))
    local = fused if (mesh.shape["gz"], mesh.shape["spec"]) == (2, 16) else gathered
    return jax.shard_map(
        local, mesh=mesh, in_specs=placed, out_specs=(P("spec", "gz"), P("spec")), check_vma=False
    )
```
